256 devices in a mesh: seq: 32 (over z, x_hi, core), tp: 8 (over y, x_lo).
Axes of the slice: x: 4 (x_hi: 2, x_lo: 2; x = x_hi * 2 + x_lo), y: 4, z: 8, core: 2. Of those that a mesh axis runs over, the one named last changes fastest.
Arguments:
- tokens: bfloat16 [12288, 4096], P('seq', 'tp'), may hold values from -6 to 6
- valid: int32 [96], P('seq'), may hold values from 1 to 128, as said below
- seg_query: bfloat16 [4096, 2048], P('seq', 'tp'), may hold values from -1 to 1
- seg_key: bfloat16 [4096, 2048], P('seq', 'tp'), may hold values from -1 to 1
- seg_value: bfloat16 [4096, 2048], P('seq', 'tp'), may hold values from -0.09375 to 0.09375
- seg_output: bfloat16 [2048, 4096], P('tp', 'seq'), may hold values from -0.125 to 0.125
- cross_query: bfloat16 [4096, 2048], P('seq', 'tp'), may hold values from -1 to 1
- cross_key: bfloat16 [4096, 2048], P('seq', 'tp'), may hold values from -1 to 1
- cross_value: bfloat16 [4096, 2048], P('seq', 'tp'), may hold values from -0.09375 to 0.09375
- cross_output: bfloat16 [2048, 4096], P('tp', 'seq'), may hold values from -0.125 to 0.125
- cotangent: bfloat16 [12288, 4096], P('seq', 'tp'), may hold values from -0.59765625 to 0.59765625
Outputs:
- layer_out: bfloat16 [12288, 4096], P('seq', 'tp')
- cross_update: float32 [96, 4096], P('seq', 'tp')
- cross_output_grad: float32 [2048, 4096], P('tp', 'seq')
The draws below stay inside these ranges and needn't reach their ends.
Inputs may be any that keep to these rules, and one draw needn't show every extreme that they name: valid[s] counts the real tokens of segment s, the first being its summary token; segments wholly inside the document hold 64 to 128 tokens, segments after the document's end hold only the summary token.
All inputs are finite; a program needn't handle non-finite values.
Results may differ from the reference program's by a relative error of at most 0.024.
Values may be sent and summed in bfloat16 or wider, within the bound.
No kernel may reach another device: no remote copies, remote signals or barrier semaphores. Data moves between devices by JAX's collectives and lax.ppermute only.
A program may use at most 64 MiB of HBM per device.

```python
import jax
import jax.numpy as jnp
from jax import lax

D = 4096
HEADS = 16
HD = 128
SEG = 128
TOKENS = 12288
SEGMENTS = 96


def draw_valid(key, part):
    key = jax.random.fold_in(key, 7)
    first, second = jax.random.split(key)
    doc_length = jax.random.randint(first, (), SEGMENTS // 2 * SEG, (SEGMENTS - 1) * SEG + 1)
    inside = jax.random.randint(second, (SEGMENTS,), SEG // 2, SEG + 1)
    index = jnp.arange(SEGMENTS)
    inside = jnp.where(index == 0, SEG, inside)
    start = index * SEG
    tail_count = jnp.clip(doc_length - start, 1, SEG)
    return jnp.where(start + SEG <= doc_length, inside, tail_count).astype(jnp.int32)


def draw_seg_query(key, part):
    key = jax.random.fold_in(key, 1)
    weight = jax.random.normal(key, (D, HEADS * HD), jnp.float32) * D ** (-0.5)
    return jnp.clip(weight, -1.0, 1.0).astype(jnp.bfloat16)


def draw_seg_key(key, part):
    key = jax.random.fold_in(key, 2)
    weight = jax.random.normal(key, (D, HEADS * HD), jnp.float32) * D ** (-0.5)
    return jnp.clip(weight, -1.0, 1.0).astype(jnp.bfloat16)


def draw_cross_query(key, part):
    key = jax.random.fold_in(key, 3)
    weight = jax.random.normal(key, (D, HEADS * HD), jnp.float32) * D ** (-0.5)
    return jnp.clip(weight, -1.0, 1.0).astype(jnp.bfloat16)


def draw_cross_key(key, part):
    key = jax.random.fold_in(key, 4)
    weight = jax.random.normal(key, (D, HEADS * HD), jnp.float32) * D ** (-0.5)
    return jnp.clip(weight, -1.0, 1.0).astype(jnp.bfloat16)


def strengthened(result, key, source, target, shards_of, factor):
    def block_of(dim):
        return (jnp.arange(result.shape[dim]) // (result.shape[dim] // shards_of)).reshape((-1,) + (1,) * (result.ndim - 1 - dim))

    one_side = jax.random.permutation(key, shards_of)[block_of(target)]
    far = (block_of(target) + shards_of // 2) % shards_of
    return jnp.where((block_of(source) == one_side) | (block_of(source) == far), factor * result, result)


def steps_of(key, dims, pieces, smallest, top_value):
    def one(dim, shards_of):
        steps = jax.random.uniform(jax.random.fold_in(jax.random.fold_in(key, 6), dim), (shards_of,), jnp.float32, smallest / len(pieces), top_value / len(pieces))
        return jnp.repeat(jnp.exp(steps), dims[dim] // shards_of).reshape((-1,) + (1,) * (len(dims) - dim - 1))

    level = one(*pieces[0])
    for cut in pieces[1:]:
        level = level * one(*cut)
    return level


def noise(rng, dims, deviation, limit, cuts=(), held_as=jnp.bfloat16):
    values = jax.random.normal(rng, dims, jnp.float32) * deviation
    if len(cuts) > 0:
        values = steps_of(rng, dims, cuts, -0.22, 0.18) * values
    return jnp.clip(values, min=-limit, max=limit).astype(held_as)


def bell_draw_with(own_key, dims, scale, bound, cuts, heavy, kind=jnp.bfloat16):
    drawn = scale * jax.random.normal(own_key, dims, jnp.float32)
    if cuts:
        drawn = drawn * steps_of(own_key, dims, cuts, -0.22, 0.18)
    return jnp.clip(strengthened(drawn, jax.random.fold_in(own_key, 3), *heavy), -bound, bound).astype(kind)


def setup_inputs(seed: int = 0) -> dict:
    seeds = jax.random.split(jax.random.key(seed), 12)
    tokens = noise(seeds[0], (TOKENS, D), 1.0, 6.0, ((0, 32), (1, 8)))
    valid = draw_valid(jax.random.fold_in(seeds[11], 71), 0)
    seg_query = draw_seg_query(jax.random.fold_in(seeds[11], 71), 0)
    seg_key = draw_seg_key(jax.random.fold_in(seeds[11], 71), 0)
    seg_value = noise(seeds[4], (D, HEADS * HD), D ** -0.5, 0.09375, ((0, 32), (1, 8)))
    seg_output = noise(seeds[5], (HEADS * HD, D), (HEADS * HD) ** -0.5, 0.125, ((0, 8), (1, 32)))
    cross_query = draw_cross_query(jax.random.fold_in(seeds[11], 71), 0)
    cross_key = draw_cross_key(jax.random.fold_in(seeds[11], 71), 0)
    cross_value = noise(seeds[8], (D, HEADS * HD), D ** -0.5, 0.09375, ((0, 32), (1, 8)))
    cross_output = noise(seeds[9], (HEADS * HD, D), (HEADS * HD) ** -0.5, 0.125, ((0, 8), (1, 32)))
    cotangent = bell_draw_with(seeds[10], (TOKENS, D), 0.1, 0.59765625, ((0, 32), (1, 8)), (0, 1, 32, 2.75))
    return dict(tokens=tokens, valid=valid, seg_query=seg_query, seg_key=seg_key, seg_value=seg_value, seg_output=seg_output, cross_query=cross_query, cross_key=cross_key, cross_value=cross_value, cross_output=cross_output, cotangent=cotangent)


def normalize(values):
    floats = values.astype(jnp.float32)
    scaled = floats * lax.rsqrt(lax.optimization_barrier(jnp.mean(floats * floats, axis=-1, keepdims=True)) + 1e-05)
    return scaled.astype(jnp.bfloat16)

def attend(query, key_rows, value_rows, allowed, scale):
    scores = jnp.einsum('bhqe,bhke->bhqk', query.astype(jnp.float32), key_rows.astype(jnp.float32)) * scale
    scores = jnp.where(allowed, scores, -1e+30)
    highest = lax.optimization_barrier(jnp.max(scores, axis=-1, keepdims=True))
    weights = jnp.exp(scores - highest)
    weights = (weights / lax.optimization_barrier(jnp.sum(weights, axis=-1, keepdims=True))).astype(jnp.bfloat16)
    mixed = jnp.einsum('bhqk,bhke->bhqe', weights.astype(jnp.float32), value_rows.astype(jnp.float32))
    return mixed.astype(jnp.bfloat16)

def reference(tokens, valid, seg_query, seg_key, seg_value, seg_output, cross_query, cross_key, cross_value, cross_output, cotangent):
    seg_count = tokens.shape[0] // SEG
    normed = normalize(tokens)
    seg_q = jnp.dot(normed, seg_query, preferred_element_type=jnp.float32).astype(jnp.bfloat16)
    seg_k = jnp.dot(normed, seg_key, preferred_element_type=jnp.float32).astype(jnp.bfloat16)
    seg_v = jnp.dot(normed, seg_value, preferred_element_type=jnp.float32).astype(jnp.bfloat16)

    def split_heads(block):
        return block.reshape(seg_count, SEG, HEADS, HD).transpose(0, 2, 1, 3)
    position = jnp.arange(SEG, dtype=jnp.int32)
    live = position[None, :] < valid[:, None]
    mixed = attend(split_heads(seg_q), split_heads(seg_k), split_heads(seg_v), live[:, None, None, :], HD ** (-0.5))
    seg_attn = mixed.transpose(0, 2, 1, 3).reshape(seg_count * SEG, HEADS * HD)
    seg_out = (tokens.astype(jnp.float32) + jnp.dot(seg_attn, seg_output, preferred_element_type=jnp.float32)).astype(jnp.bfloat16)
    summary = seg_out.reshape(seg_count, SEG, D)[:, 0]
    summary_normed = normalize(summary)
    cross_q = jnp.dot(summary_normed, cross_query, preferred_element_type=jnp.float32).astype(jnp.bfloat16)
    cross_k = jnp.dot(summary_normed, cross_key, preferred_element_type=jnp.float32).astype(jnp.bfloat16)
    cross_v = jnp.dot(summary_normed, cross_value, preferred_element_type=jnp.float32).astype(jnp.bfloat16)

    def heads_first(block):
        return block.reshape(seg_count, HEADS, HD).transpose(1, 0, 2)[None]
    cross_mixed = attend(heads_first(cross_q), heads_first(cross_k), heads_first(cross_v), True, HD ** (-0.5))[0]
    cross_attn = cross_mixed.transpose(1, 0, 2).reshape(seg_count, HEADS * HD)
    cross_update = jnp.dot(cross_attn, cross_output, preferred_element_type=jnp.float32)
    row_keep = live.astype(jnp.float32)[:, :, None]
    layer_out = (seg_out.astype(jnp.float32).reshape(seg_count, SEG, D) + cross_update[:, None, :]) * row_keep
    layer_out = layer_out.reshape(seg_count * SEG, D).astype(jnp.bfloat16)
    seg_grad = lax.optimization_barrier(jnp.sum(cotangent.astype(jnp.float32).reshape(seg_count, SEG, D) * row_keep, axis=1)).astype(jnp.bfloat16)
    cross_output_grad = jnp.dot(cross_attn.T, seg_grad, preferred_element_type=jnp.float32)
    return (layer_out, cross_update, cross_output_grad)
```

```python
import jax
import jax.numpy as jnp
from jax import lax
from jax.experimental import pallas as pl
from jax.experimental.pallas import tpu as pltpu
from jax.sharding import PartitionSpec as P

HD = 128
SEG = 128
EPS = 1e-05
NZ = 8
NY = 4
BF = jnp.bfloat16
F32 = jnp.float32
VMEM = pl.BlockSpec(memory_space=pltpu.VMEM)
SMEM = pl.BlockSpec(memory_space=pltpu.SMEM)

CORE = [(i, i ^ 1) for i in range(32)]
XHI = [(i, i ^ 2) for i in range(32)]
XLO = [(i, i ^ 1) for i in range(8)]


def along_z(step):
    return [(i, (i + 4 * step) % 32) for i in range(32)]


def along_y(step):
    return [(i, (i + 2 * step) % 8) for i in range(8)]


def call(body, outs, args, scratch=(), flops=0, moved=0):
    specs = [SMEM if a.dtype == jnp.int32 else VMEM for a in args]
    return pl.pallas_call(
        body,
        out_shape=outs,
        in_specs=specs,
        out_specs=[VMEM] * len(outs),
        scratch_shapes=list(scratch),
        compiler_params=pltpu.CompilerParams(vmem_limit_bytes=40 * 2**20),
        cost_estimate=pl.CostEstimate(flops=flops, bytes_accessed=moved, transcendentals=0),
    )(*args)


def shape(dims, dtype):
    return jax.ShapeDtypeStruct(dims, dtype)


def dot(a, b):
    return jnp.dot(a, b, preferred_element_type=F32)


def z_ring(own, half):
    up = down = own
    pieces = {0: own}
    for k in range(1, 4):
        up = lax.ppermute(up, "seq", along_z(1))
        down = lax.ppermute(down, "seq", along_z(-1))
        pieces[NZ - k] = up
        pieces[k] = down
    first = lax.ppermute(half(up, 0), "seq", along_z(1))
    second = lax.ppermute(half(down, 1), "seq", along_z(-1))
    return [pieces[0], pieces[1], pieces[2], pieces[3], first, second, pieces[5], pieces[6], pieces[7]]


def gather_rows(block, x_hi):
    other = lax.ppermute(block, "seq", XHI)
    plane = jnp.concatenate(
        [jnp.where(x_hi == 0, block, other), jnp.where(x_hi == 0, other, block)], axis=0
    )
    rows = block.shape[0]
    return z_ring(plane, lambda p, h: p[h * rows : (h + 1) * rows])


def gather_cols(block, x_hi):
    other = lax.ppermute(block, "seq", XHI)
    plane = jnp.concatenate(
        [jnp.where(x_hi == 0, block, other), jnp.where(x_hi == 0, other, block)], axis=1
    )
    cols = block.shape[1]
    return z_ring(plane, lambda p, h: p[:, h * cols : (h + 1) * cols])


def assemble_kernel(pos, p0, p1, p2a, p2b, p3, x_out, own_sq, sib_sq, first_rows):
    core, y = pos[2], pos[3]
    rows = p0.shape[1]
    per = rows // 2
    x_out[0:2] = p0[...]
    x_out[2:4] = p1[...]
    x_out[4] = p2a[...]
    x_out[5] = p2b[...]
    x_out[6:8] = p3[...]
    segs = per // SEG
    for which, ref in ((0, own_sq), (1, sib_sq)):
        base = pl.multiple_of((core if which == 0 else 1 - core) * per, per)
        for j in range(segs):
            at = pl.ds(base + j * SEG, SEG)
            total = jnp.zeros((SEG, 128), F32)
            for k in range(8):
                v = x_out[k, at, :].astype(F32)
                total += v[:, :128] * v[:, :128] + v[:, 128:] * v[:, 128:]
            ref[j * SEG : (j + 1) * SEG, :] = jnp.broadcast_to(
                jnp.sum(total, axis=1, keepdims=True), (SEG, 128)
            )
    first_rows[...] = jnp.zeros_like(first_rows)
    for k in range(8):
        t = lax.rem(k + 2 * y, 8)
        for r in range(2 * segs):
            first_rows[t, r : r + 1, :] = x_out[k, r * SEG : r * SEG + 16, :].astype(F32)[0:1]


def project_kernel(pos, x, *refs):
    w, (own, sib) = refs[:9], refs[9:]
    z, core, y = pos[0], pos[2], pos[3]
    per = own.shape[0]
    half = w[4].shape[0]
    tile = SEG
    for which, ref in ((1, sib), (0, own)):
        base = pl.multiple_of((core if which == 0 else 1 - core) * per, per)
        for j in range(per // tile):
            at = pl.ds(base + j * tile, tile)
            total = None
            for k in range(8):
                index = lax.rem(z + k - 2 * y + 16, 8)
                rows = x[index, at, :]
                if k == 4:
                    term = dot(rows[:, :half], w[4][...]) + dot(rows[:, half:], w[5][...])
                else:
                    term = dot(rows, w[k if k < 4 else k + 1][...])
                total = term if total is None else total + term
            ref[j * tile : (j + 1) * tile, :] = total.astype(ref.dtype)


def attend_kernel(valid, own, got, own_sq, got_sq, mixed):
    heads = mixed.shape[1] // HD
    width = heads * HD
    features = 4096.0
    for j in range(own.shape[0] // SEG):
        at = slice(j * SEG, (j + 1) * SEG)
        scale = lax.rsqrt((own_sq[at, :] + got_sq[at, :]) * (1.0 / features) + EPS)
        allowed = lax.broadcasted_iota(jnp.int32, (SEG, SEG), 1) < valid[j]
        for h in range(heads):
            parts = []
            for kind in range(3):
                cols = slice(kind * width + h * HD, kind * width + (h + 1) * HD)
                parts.append(((own[at, cols] + got[at, cols].astype(F32)) * scale).astype(BF))
            q, k, v = parts
            scores = lax.dot_general(
                q, k, (((1,), (1,)), ((), ())), preferred_element_type=F32
            ) * (HD**-0.5)
            scores = jnp.where(allowed, scores, -1e30)
            weights = jnp.exp(scores - jnp.max(scores, axis=1, keepdims=True))
            weights = (weights / jnp.sum(weights, axis=1, keepdims=True)).astype(BF)
            mixed[at, h * HD : (h + 1) * HD] = dot(weights, v).astype(BF)


def out_kernel(pos, own, got, *refs):
    w, outs, summary, table = refs[:9], refs[9:17], refs[17], refs[18]
    z, core, y, x_lo = pos[0], pos[2], pos[3], pos[4]
    per = own.shape[0]
    segs = per // SEG
    half = w[4].shape[1]
    for k in range(8):
        if k == 4:
            table[4, :, :half] = w[4][...]
            table[4, :, half:] = w[5][...]
        else:
            table[k] = w[k if k < 4 else k + 1][...]
    summary[...] = jnp.zeros_like(summary)
    for dy in range(4):
        for dx in range(2):
            t = lax.rem(y + dy, 4) * 2 + (x_lo + dx) % 2
            piece = table[lax.rem(t - z + 8, 8)]
            ref = outs[dy * 2 + dx]
            for which, src in ((0, own), (1, got)):
                chip_core = core if which == 0 else 1 - core
                base = pl.multiple_of(chip_core * per, per)
                for j in range(segs):
                    part = dot(src[j * SEG : (j + 1) * SEG, :], piece)
                    ref[pl.ds(base + j * SEG, SEG), :] = part.astype(BF)
                    summary[t, pl.ds(chip_core * segs + j, 1), :] = part[0:1]


def cross_project_kernel(pos, first_rows, sums, *refs):
    w, out = refs[:9], refs[9]
    z = pos[0]
    half = w[4].shape[0]
    total = jnp.zeros((8, w[0].shape[1]), F32)
    square = jnp.zeros((8, 128), F32)
    for k in range(8):
        t = lax.rem(z + k, 8)
        rows = (first_rows[t] + sums[t]).astype(BF)
        wide = rows.astype(F32)
        square += wide[:, :128] * wide[:, :128] + wide[:, 128:] * wide[:, 128:]
        if k == 4:
            total += dot(rows[:, :half], w[4][...]) + dot(rows[:, half:], w[5][...])
        else:
            total += dot(rows, w[k if k < 4 else k + 1][...])
    out[:, : total.shape[1]] = total
    out[:, total.shape[1] :] = jnp.broadcast_to(jnp.sum(square, axis=1, keepdims=True), (8, 128))


def cross_scale_kernel(own, got, out):
    width = own.shape[1] - 128
    scale = lax.rsqrt((own[:, width:] + got[:, width:]) * (1.0 / 4096.0) + EPS)
    for k in range(width // 128):
        cols = slice(k * 128, (k + 1) * 128)
        out[:, cols] = (own[:, cols] + got[:, cols]) * scale


def cross_attend_kernel(pos, *refs):
    blocks, w, (update, mixed, table) = refs[:8], refs[8:17], refs[17:]
    x_hi, z = pos[1], pos[0]
    rows = jnp.concatenate([b[...] for b in blocks], axis=0)
    count = rows.shape[0]
    width = rows.shape[1] // 3
    key_index = lax.broadcasted_iota(jnp.int32, (count, count), 1)
    allowed = key_index % 8 < 6
    for h in range(width // HD):
        q = rows[:, h * HD : (h + 1) * HD]
        k = rows[:, width + h * HD : width + (h + 1) * HD]
        v = rows[:, 2 * width + h * HD : 2 * width + (h + 1) * HD]
        scores = lax.dot_general(
            q, k, (((1,), (1,)), ((), ())), preferred_element_type=F32
        ) * (HD**-0.5)
        scores = jnp.where(allowed, scores, -1e30)
        weights = jnp.exp(scores - jnp.max(scores, axis=1, keepdims=True))
        weights = (weights / jnp.sum(weights, axis=1, keepdims=True)).astype(BF)
        table[:, h * HD : (h + 1) * HD] = dot(weights, v)
    mixed[...] = table[...].astype(BF)
    mine = table[pl.ds(pl.multiple_of(x_hi * 8, 8), 8), :].astype(BF)
    half = w[4].shape[1]
    for k in range(8):
        t = lax.rem(z + k, 8)
        if k == 4:
            update[t, :, :half] = dot(mine, w[4][...])
            update[t, :, half:] = dot(mine, w[5][...])
        else:
            update[t] = dot(mine, w[k if k < 4 else k + 1][...])


def grad_kernel(pos, mixed, grads, out, table):
    z, t = pos[0], pos[3] * 2 + pos[4]
    for k in range(8):
        delta = (0, 1, 2, 3, 4, 5, 6, 7)[k]
        table[lax.rem(z + delta, 8)] = mixed[k * 16 : (k + 1) * 16, :]
    total = jnp.zeros(out.shape, F32)
    for k in range(8):
        left = table[t ^ k]
        total += lax.dot_general(
            left, grads[k * 16 : (k + 1) * 16, :], (((0,), (0,)), ((), ())),
            preferred_element_type=F32,
        )
    out[...] = total


def local(
    tokens, valid, seg_query, seg_key, seg_value, seg_output,
    cross_query, cross_key, cross_value, cross_output, cotangent,
):
    per, cols = tokens.shape
    segs = per // SEG
    s = lax.axis_index("seq")
    t = lax.axis_index("tp")
    z, x_hi, core = s // 4, (s // 2) % 2, s % 2
    y, x_lo = t // 2, t % 2
    pos = jnp.stack([z, x_hi, core, y, x_lo]).astype(jnp.int32)
    is0 = core == 0

    four = tokens.reshape(per, 2, 2, 128)
    keep = jnp.where(is0, four[:, :, 0], four[:, :, 1]).reshape(per, 256)
    give = jnp.where(is0, four[:, :, 1], four[:, :, 0]).reshape(per, 256)
    take = lax.ppermute(give, "seq", CORE)
    chip = jnp.concatenate([jnp.where(is0, keep, take), jnp.where(is0, take, keep)], axis=0)

    qkv = gather_rows(jnp.concatenate([seg_query, seg_key, seg_value], axis=1), x_hi)

    chip_x = lax.ppermute(chip, "tp", XLO)
    p0 = jnp.stack([jnp.where(x_lo == 0, chip, chip_x), jnp.where(x_lo == 0, chip_x, chip)])
    p3 = lax.ppermute(p0, "tp", along_y(1))
    p1 = lax.ppermute(p0, "tp", along_y(-1))
    p2a = lax.ppermute(p3[0], "tp", along_y(1))
    p2b = lax.ppermute(p1[1], "tp", along_y(-1))

    out_w = gather_cols(seg_output, x_hi)
    cross_w = gather_rows(jnp.concatenate([cross_query, cross_key, cross_value], axis=1), x_hi)
    cross_out_w = gather_cols(cross_output, x_hi)

    x, own_sq, sib_sq, first_rows = call(
        assemble_kernel,
        [
            shape((8, 2 * per, 256), BF),
            shape((per, 128), F32),
            shape((per, 128), F32),
            shape((8, 8, 256), F32),
        ],
        (pos, p0, p1, p2a, p2b, p3),
        moved=8 * 2**20,
    )
    got_sq = lax.ppermute(sib_sq, "seq", CORE)
    own_p, sib_p = call(
        project_kernel,
        [shape((per, 768), F32), shape((per, 768), BF)],
        (pos, x, *qkv),
        flops=2 * 768 * 768 * 2048,
        moved=8 * 2**20,
    )
    got_p = lax.ppermute(sib_p, "seq", CORE)
    (mixed,) = call(
        attend_kernel,
        [shape((per, 256), BF)],
        (valid, own_p, got_p, own_sq, got_sq),
        flops=10**8,
        moved=3 * 2**20,
    )
    mixed_sib = lax.ppermute(mixed, "seq", CORE)
    *outs, summary = call(
        out_kernel,
        [shape((2 * per, 256), BF)] * 8 + [shape((8, 8, 256), F32)],
        (pos, mixed, mixed_sib, *out_w),
        scratch=[pltpu.VMEM((8, 256, 256), BF)],
        flops=2 * 768 * 256 * 2048,
        moved=5 * 2**20,
    )
    for bit in (1, 2, 4):
        summary = summary + lax.ppermute(summary, "tp", [(i, i ^ bit) for i in range(8)])

    total = outs[0].astype(F32)
    for dy in range(4):
        for dx in range(2):
            if dy or dx:
                pairs = [(i, ((i // 2 + dy) % 4) * 2 + ((i % 2) ^ dx)) for i in range(8)]
                total = total + lax.ppermute(outs[dy * 2 + dx], "tp", pairs).astype(F32)
    seg_half = (chip.astype(F32) + total).astype(BF)
    top, bottom = seg_half[:per], seg_half[per:]
    mine_half = jnp.where(is0, top, bottom)
    their_half = lax.ppermute(jnp.where(is0, bottom, top), "seq", CORE)

    def both_columns(mine, theirs):
        a = jnp.where(is0, mine, theirs).reshape(-1, 2, 1, 128)
        b = jnp.where(is0, theirs, mine).reshape(-1, 2, 1, 128)
        return jnp.concatenate([a, b], axis=2).reshape(-1, 512)

    seg_out = both_columns(mine_half, their_half)

    (cross_part,) = call(
        cross_project_kernel, [shape((8, 896), F32)], (pos, first_rows, summary, *cross_w),
        flops=10**8, moved=3 * 2**20,
    )
    cross_got = lax.ppermute(cross_part, "seq", CORE)
    (chip_qkv,) = call(cross_scale_kernel, [shape((8, 768), F32)], (cross_part, cross_got), moved=10**5)
    chip_other = lax.ppermute(chip_qkv, "seq", XHI)
    plane = jnp.concatenate(
        [jnp.where(x_hi == 0, chip_qkv, chip_other), jnp.where(x_hi == 0, chip_other, chip_qkv)]
    ).astype(BF)
    blocks = [plane] + [lax.ppermute(plane, "seq", along_z(-k)) for k in range(1, 8)]
    update, cross_mixed = call(
        cross_attend_kernel,
        [shape((8, 8, 256), F32), shape((128, 256), BF)],
        (pos, *blocks, *cross_out_w),
        scratch=[pltpu.VMEM((128, 256), F32)],
        flops=10**8,
        moved=2 * 2**20,
    )
    for bit in (1, 2, 4):
        update = update + lax.ppermute(update, "tp", [(i, i ^ bit) for i in range(8)])
    mine_update = lax.dynamic_index_in_dim(update, t, 0, keepdims=False)
    low, high = mine_update[:segs], mine_update[segs : 2 * segs]
    their_update = lax.ppermute(jnp.where(is0, high, low), "seq", CORE)
    cross_update = both_columns(jnp.where(is0, low, high), their_update)

    live = jnp.arange(SEG, dtype=jnp.int32)[None, :] < valid[:, None]
    keep_rows = live.astype(F32)[:, :, None]
    layer_out = (seg_out.astype(F32).reshape(segs, SEG, cols) + cross_update[:, None, :]) * keep_rows
    layer_out = layer_out.reshape(per, cols).astype(BF)

    grad = jnp.sum(cotangent.astype(F32).reshape(segs, SEG, cols) * keep_rows, axis=1)
    grad = grad.astype(BF).reshape(segs, 2, 2, 128)
    g_keep = jnp.where(is0, grad[:, :, 0], grad[:, :, 1])
    g_take = lax.ppermute(jnp.where(is0, grad[:, :, 1], grad[:, :, 0]), "seq", CORE)
    g_chip = jnp.concatenate(
        [jnp.where(is0, g_keep, g_take), jnp.where(is0, g_take, g_keep), jnp.zeros((2, 2, 128), BF)]
    )
    g_keep = jnp.where(x_hi == 0, g_chip[:, 0], g_chip[:, 1])
    g_take = lax.ppermute(jnp.where(x_hi == 0, g_chip[:, 1], g_chip[:, 0]), "seq", XHI)
    g_rows = jnp.concatenate([jnp.where(x_hi == 0, g_keep, g_take), jnp.where(x_hi == 0, g_take, g_keep)])
    for bit in (1, 2, 4):
        more = lax.ppermute(g_rows, "seq", [(i, i ^ (4 * bit)) for i in range(32)])
        g_rows = jnp.concatenate([g_rows, more])
    swap = []
    for i in range(32):
        for j in range(8):
            swap.append((i * 8 + j, (j * 4 + i % 4) * 8 + i // 4))
    g_mine = lax.ppermute(g_rows, ("seq", "tp"), swap)
    (grad_weight,) = call(
        grad_kernel, [shape((256, 128), F32)], (pos, cross_mixed, g_mine),
        scratch=[pltpu.VMEM((8, 16, 256), BF)], flops=10**7, moved=10**5,
    )
    return (layer_out, cross_update, grad_weight)


def solution(mesh):
    return jax.shard_map(
        local,
        mesh=mesh,
        in_specs=(
            P("seq", "tp"),
            P("seq"),
            P("seq", "tp"),
            P("seq", "tp"),
            P("seq", "tp"),
            P("tp", "seq"),
            P("seq", "tp"),
            P("seq", "tp"),
            P("seq", "tp"),
            P("tp", "seq"),
            P("seq", "tp"),
        ),
        out_specs=(P("seq", "tp"), P("seq", "tp"), P("tp", "seq")),
        check_vma=False,
    )
```

```python
import jax
import jax.numpy as jnp
from jax import lax
from jax.experimental import pallas as pl
from jax.experimental.pallas import tpu as pltpu
from jax.sharding import PartitionSpec as P

HD = 128
SEG = 128
EPS = 1e-05
NZ = 8
NY = 4
BF = jnp.bfloat16
F32 = jnp.float32
VMEM = pl.BlockSpec(memory_space=pltpu.VMEM)
SMEM = pl.BlockSpec(memory_space=pltpu.SMEM)

CORE = [(i, i ^ 1) for i in range(32)]
XHI = [(i, i ^ 2) for i in range(32)]
XLO = [(i, i ^ 1) for i in range(8)]


def along_z(step):
    return [(i, (i + 4 * step) % 32) for i in range(32)]


def along_y(step):
    return [(i, (i + 2 * step) % 8) for i in range(8)]


def call(body, outs, args, scratch=(), flops=0, moved=0):
    specs = [SMEM if a.dtype == jnp.int32 else VMEM for a in args]
    return pl.pallas_call(
        body,
        out_shape=outs,
        in_specs=specs,
        out_specs=[VMEM] * len(outs),
        scratch_shapes=list(scratch),
        compiler_params=pltpu.CompilerParams(vmem_limit_bytes=16 * 2**20),
        cost_estimate=pl.CostEstimate(flops=flops, bytes_accessed=moved, transcendentals=0),
    )(*args)


def shape(dims, dtype):
    return jax.ShapeDtypeStruct(dims, dtype)


def dot(a, b):
    return jnp.dot(a, b, preferred_element_type=F32)


def tie(*arrays):
    return lax.optimization_barrier(arrays)


def in_order(flag, mine, other, axis):
    return jnp.concatenate(
        [jnp.where(flag, mine, other), jnp.where(flag, other, mine)], axis=axis
    )


def assemble_kernel(pos, p0, p1, p2a, p2b, p3, x_out, own_sq, sib_sq):
    core, y = pos[2], pos[3]
    rows = p0.shape[1]
    per = rows // 2
    x_out[0:2] = p0[...]
    x_out[2:4] = p1[...]
    x_out[4] = p2a[...]
    x_out[5] = p2b[...]
    x_out[6:8] = p3[...]
    segs = per // SEG
    for which, ref in ((0, own_sq), (1, sib_sq)):
        base = pl.multiple_of((core if which == 0 else 1 - core) * per, per)
        for j in range(segs):
            at = pl.ds(base + j * SEG, SEG)
            total = jnp.zeros((SEG, 128), F32)
            for k in range(8):
                v = x_out[k, at, :].astype(F32)
                total += v[:, :128] * v[:, :128] + v[:, 128:] * v[:, 128:]
            ref[j * SEG : (j + 1) * SEG, :] = jnp.broadcast_to(
                jnp.sum(total, axis=1, keepdims=True), (SEG, 128)
            )


def project_kernel(pos, x, *refs):
    w, (own, sib) = refs[:9], refs[9:]
    z, core, y = pos[0], pos[2], pos[3]
    per, width = own.shape
    half = w[4].shape[1]
    tile = SEG
    for which, ref in ((1, sib), (0, own)):
        base = pl.multiple_of((core if which == 0 else 1 - core) * per, per)
        for j in range(per // tile):
            at = pl.ds(base + j * tile, tile)
            total = None
            for k in range(8):
                index = lax.rem(z + k - 2 * y + 16, 8)
                rows = x[index, at, :]
                if k == 4:
                    term = jnp.concatenate(
                        [dot(rows, w[4][...]), dot(rows, w[5][:, : width - half])], axis=1
                    )
                else:
                    term = dot(rows, w[k if k < 4 else k + 1][:, :width])
                total = term if total is None else total + term
            ref[j * tile : (j + 1) * tile, :] = total.astype(ref.dtype)


def attend_kernel(valid, own, got, own_sq, got_sq, out, mixed):
    heads = mixed.shape[1] // HD
    width = heads * HD
    features = 4096.0
    for j in range(own.shape[0] // SEG):
        at = slice(j * SEG, (j + 1) * SEG)
        scale = lax.rsqrt((own_sq[at, :] + got_sq[at, :]) * (1.0 / features) + EPS)
        allowed = lax.broadcasted_iota(jnp.int32, (SEG, SEG), 1) < valid[j]
        for h in range(heads):
            parts = []
            for kind in range(3):
                cols = slice(kind * width + h * HD, kind * width + (h + 1) * HD)
                parts.append(((own[at, cols] + got[at, cols].astype(F32)) * scale).astype(BF))
            q, k, v = parts
            scores = lax.dot_general(
                q, k, (((1,), (1,)), ((), ())), preferred_element_type=F32
            ) * (HD**-0.5)
            scores = jnp.where(allowed, scores, -1e30)
            weights = jnp.exp(scores - jnp.max(scores, axis=1, keepdims=True))
            weights = (weights / jnp.sum(weights, axis=1, keepdims=True)).astype(BF)
            part = dot(weights, v).astype(BF)
            mixed[at, h * HD : (h + 1) * HD] = part
    for to in range(out.shape[0]):
        out[to] = mixed[...]


def out_kernel(pos, chip, own, sib, grads, *refs):
    w, (mine, theirs, summary, rows) = refs[:9], refs[9:]
    z, core = pos[0], pos[2]
    per = mine.shape[0]
    part = per // 2
    segs = per // SEG
    rows[...] = jnp.zeros_like(rows)
    for which, src, ref in ((0, own, mine), (1, sib, theirs)):
        chip_core = core if which == 0 else 1 - core
        for h in range(2):
            at = slice(h * part, (h + 1) * part)
            total = None
            for k in range(8):
                weights = w[k if k < 4 else k + 1]
                last = weights.shape[1]
                term = dot(src[lax.rem(z + k, 8), at, :], weights[:, last - 256 : last])
                total = term if total is None else total + term
            base = pl.multiple_of(chip_core * per + h * part, part)
            sums = (chip[pl.ds(base, part), :].astype(F32) + total).astype(BF)
            ref[at, :] = sums
            for j in range(segs):
                place = j * SEG - h * part
                if 0 <= place < part:
                    row = sums[place : place + 16, :].astype(F32)[0:1]
                    rows[pl.ds(chip_core * segs + j, 1), :] = row
    for to in range(summary.shape[0]):
        summary[to, 0:8, :] = rows[...]
        summary[to, 8:16, :] = grads[...]


def cross_project_kernel(pos, rows, *refs):
    w, out, table = refs[:9], refs[9], refs[10]
    z = pos[0]
    width = out.shape[1] - 128
    half = w[4].shape[1]
    total = jnp.zeros((8, width), F32)
    square = jnp.zeros((8, 128), F32)
    for k in range(8):
        at = lax.rem(z + k, 8)
        wide = rows[at, 0:8, :]
        ref = w[k if k < 4 else k + 1]
        table[at] = ref[:, ref.shape[1] - 512 : ref.shape[1] - 256]
        square += wide[:, :128] * wide[:, :128] + wide[:, 128:] * wide[:, 128:]
        wide = wide.astype(BF)
        if k == 4:
            total += jnp.concatenate(
                [dot(wide, w[4][...]), dot(wide, w[5][:, : width - half])], axis=1
            )
        else:
            total += dot(wide, ref[:, :width])
    out[:, :width] = total
    out[:, width:] = jnp.broadcast_to(jnp.sum(square, axis=1, keepdims=True), (8, 128))


def cross_scale_kernel(own, got, out):
    width = own.shape[1] - 128
    scale = lax.rsqrt((own[:, width:] + got[:, width:]) * (1.0 / 4096.0) + EPS)
    for k in range(width // 128):
        cols = slice(k * 128, (k + 1) * 128)
        block = ((own[:, cols] + got[:, cols]) * scale).astype(BF)
        for to in range(out.shape[0]):
            out[to, :, cols] = block


def cross_attend_kernel(pos, gathered, w, mixed, update, table):
    z, x_hi = pos[0], pos[1]
    count = gathered.shape[0] * 8
    rows = gathered[...].astype(F32).reshape(count, gathered.shape[2]).astype(BF)
    width = rows.shape[1] // 3
    key_index = lax.broadcasted_iota(jnp.int32, (count, count), 1)
    allowed = key_index % 8 < 6
    for h in range(width // HD):
        q = rows[:, h * HD : (h + 1) * HD]
        k = rows[:, width + h * HD : width + (h + 1) * HD]
        v = rows[:, 2 * width + h * HD : 2 * width + (h + 1) * HD]
        scores = lax.dot_general(
            q, k, (((1,), (1,)), ((), ())), preferred_element_type=F32
        ) * (HD**-0.5)
        scores = jnp.where(allowed, scores, -1e30)
        weights = jnp.exp(scores - jnp.max(scores, axis=1, keepdims=True))
        weights = (weights / jnp.sum(weights, axis=1, keepdims=True)).astype(BF)
        table[:, h * HD : (h + 1) * HD] = dot(weights, v)
    mixed[...] = table[...].astype(BF)
    chip = table[pl.ds(pl.multiple_of((z * 2 + x_hi) * 8, 8), 8), :].astype(BF)
    for k in range(8):
        update[k] = dot(chip, w[k])


def update_kernel(pos, parts, mine, theirs):
    core = pos[2]
    total = parts[0]
    for k in range(1, parts.shape[0]):
        total = total + parts[k]
    later = jnp.concatenate([total[3:], total[:3]], axis=0)
    mine[...] = jnp.where(core == 0, total, later)
    theirs[...] = jnp.where(core == 0, later, total)


def final_kernel(pos, valid, seg_mine, seg_theirs, mine, theirs, out, update):
    core = pos[2]
    segs = update.shape[0]
    place = lax.broadcasted_iota(jnp.int32, (SEG, 1), 0)
    for which, seg, ref in ((0, seg_mine, mine), (1, seg_theirs, theirs)):
        part = core if which == 0 else 1 - core
        for x in range(2):
            cols = pl.ds(pl.multiple_of(x * 256 + part * 128, 128), 128)
            from_cols = slice(x * 128, (x + 1) * 128)
            update[:, cols] = ref[:segs, from_cols]
            for j in range(segs):
                at = slice(j * SEG, (j + 1) * SEG)
                live = (place < valid[j]).astype(F32)
                sums = seg[at, from_cols].astype(F32) + ref[j : j + 1, from_cols]
                out[at, cols] = (sums * live).astype(BF)


def grad_kernel(mixed, grads, out):
    total = jnp.zeros(out.shape, F32)
    for k in range(8):
        block = grads[k, 8:16, :]
        right = jnp.concatenate([block[:, :128], block[:, 128:]], axis=0).astype(BF)
        total += lax.dot_general(
            mixed[k * 16 : (k + 1) * 16, :], right, (((0,), (0,)), ((), ())),
            preferred_element_type=F32,
        )
    out[...] = total


def local(
    tokens, valid, seg_query, seg_key, seg_value, seg_output,
    cross_query, cross_key, cross_value, cross_output, cotangent,
):
    per, cols = tokens.shape
    segs = per // SEG
    s = lax.axis_index("seq")
    t = lax.axis_index("tp")
    z, x_hi, core = s // 4, (s // 2) % 2, s % 2
    y, x_lo = t // 2, t % 2
    pos = jnp.stack([z, x_hi, core, y, x_lo]).astype(jnp.int32)
    is0 = core == 0

    at0 = x_hi == 0
    low = x_lo == 0
    swap = [
        (i * 8 + j, (j * 4 + i % 4) * 8 + i // 4) for i in range(32) for j in range(8)
    ]


    def z_step(block, step):
        return lax.ppermute(block, "seq", along_z(step))

    def y_step(block, step):
        return lax.ppermute(block, "tp", along_y(step))

    four = tokens.reshape(per, 2, 2, 128)
    keep = jnp.where(is0, four[:, :, 0], four[:, :, 1]).reshape(per, 256)
    give = jnp.where(is0, four[:, :, 1], four[:, :, 0]).reshape(per, 256)
    block = jnp.concatenate([seg_query, seg_key, seg_value], axis=1)
    cross_block = jnp.concatenate([cross_query, cross_key, cross_value], axis=1)
    far = lax.ppermute(block, "seq", XHI)
    take = lax.ppermute(give, "seq", CORE)
    live = jnp.arange(SEG, dtype=jnp.int32)[None, :] < valid[:, None]
    keep_rows = live.astype(F32)[:, :, None]
    grad = jnp.sum(cotangent.astype(F32).reshape(segs, SEG, cols) * keep_rows, axis=1)
    grad = jnp.pad(grad.astype(BF), ((0, 1), (0, 0))).reshape(16, 128)
    turned = lax.ppermute(jnp.concatenate([seg_output, grad], axis=0), ("seq", "tp"), swap)
    far, take = tie(far, take)

    plane = in_order(at0, block, far, 0)
    chip = in_order(is0, keep, take, 0)
    chip_x = lax.ppermute(chip, "tp", XLO)
    up1, down1 = z_step(plane, 1), z_step(plane, -1)
    up1, down1, chip_x, turned, cross_block, cross_output = tie(
        up1, down1, chip_x, turned, cross_block, cross_output
    )

    up2, down2 = z_step(up1, 1), z_step(down1, -1)
    p0 = in_order(low, chip[None], chip_x[None], 0)
    p3, p1 = y_step(p0, 1), y_step(p0, -1)
    grad = turned[256:].reshape(segs + 1, 2, 2, 128)[:segs]
    g_keep = jnp.where(is0, grad[:, :, 0], grad[:, :, 1])
    g_take = lax.ppermute(jnp.where(is0, grad[:, :, 1], grad[:, :, 0]), "seq", CORE)
    cross_pack = jnp.concatenate(
        [cross_block, cross_output[:128], cross_output[128:], turned[:128], turned[128:256]],
        axis=1,
    )
    cross_far = lax.ppermute(cross_pack, "seq", XHI)
    up2, down2, cross_far, g_take = tie(up2, down2, cross_far, g_take)

    up3, down3 = z_step(up2, 1), z_step(down2, -1)
    g_chip = jnp.concatenate(
        [in_order(is0, g_keep, g_take, 0), jnp.zeros((8 - 2 * segs, 2, 128), BF)]
    )
    g_own = jnp.where(at0, g_chip[:, 0], g_chip[:, 1])
    g_far = lax.ppermute(jnp.where(at0, g_chip[:, 1], g_chip[:, 0]), "seq", XHI)
    g_rows = in_order(at0, g_own, g_far, 1).astype(F32)

    def tall(wide):
        return jnp.concatenate([wide[:, :128], wide[:, 128:]], axis=0)

    cross_plane = jnp.concatenate(
        [
            in_order(at0, cross_block, cross_far[:, :768], 0),
            in_order(at0, cross_output, tall(cross_far[:, 768:1024]), 1),
            in_order(at0, turned[:256], tall(cross_far[:, 1024:]), 1),
        ],
        axis=1,
    )
    up3, down3, cross_plane, g_rows = tie(up3, down3, cross_plane, g_rows)

    half = plane.shape[1] // 2
    up4, down4 = z_step(up3[:, :half], 1), z_step(down3[:, half:], -1)
    p2a, p2b = y_step(p3[0], 1), y_step(p1[1], -1)
    p2a, cross_plane = tie(p2a, cross_plane)
    c_up1, c_down1 = z_step(cross_plane, 1), z_step(cross_plane, -1)
    up4, down4, p2a, p2b = tie(up4, down4, p2a, p2b)

    x, own_sq, sib_sq = call(
        assemble_kernel,
        [shape((8, 2 * per, 256), BF), shape((per, 128), F32), shape((per, 128), F32)],
        (pos, p0, p1, p2a, p2b, p3),
        moved=8 * 2**20,
    )
    got_sq = lax.ppermute(sib_sq, "seq", CORE)
    own_p, sib_p = call(
        project_kernel,
        [shape((per, 768), F32), shape((per, 768), BF)],
        (pos, x, plane, down1, down2, down3, up4, down4, up3, up2, up1),
        flops=2 * 768 * 768 * 2048,
        moved=8 * 2**20,
    )
    got_p = lax.ppermute(sib_p, "seq", CORE)
    got_p, got_sq, c_up1, c_down1 = tie(got_p, got_sq, c_up1, c_down1)
    c_up2, c_down2 = z_step(c_up1, 1), z_step(c_down1, -1)
    (mixed,) = call(
        attend_kernel,
        [shape((8, per, 256), BF)],
        (valid, own_p, got_p, own_sq, got_sq),
        scratch=[pltpu.VMEM((per, 256), BF)],
        flops=10**8,
        moved=3 * 2**20,
    )

    mixed, c_up2, c_down2 = tie(mixed, c_up2, c_down2)
    c_up3, c_down3 = z_step(c_up2, 1), z_step(c_down2, -1)
    mixed = lax.all_to_all(mixed, "tp", 0, 0)
    mixed, c_up3, c_down3 = tie(mixed, c_up3, c_down3)
    half = cross_plane.shape[1] // 2
    c_up4, c_down4 = z_step(c_up3[:, :half], 1), z_step(c_down3[:, half:], -1)
    cross_w = (
        cross_plane, c_down1, c_down2, c_down3, c_up4, c_down4, c_up3, c_up2, c_up1
    )
    mixed_sib = lax.ppermute(mixed, "seq", CORE)
    seg_mine, seg_give, summary = call(
        out_kernel,
        [shape((per, 256), BF), shape((per, 256), BF), shape((8, 16, 256), F32)],
        (pos, chip, mixed, mixed_sib, g_rows, *cross_w),
        scratch=[pltpu.VMEM((8, 256), F32)],
        flops=2 * per * 512 * 2048,
        moved=6 * 2**20,
    )
    summaries = lax.all_to_all(summary, "tp", 0, 0)
    seg_take = lax.ppermute(seg_give, "seq", CORE)

    cross_part, back_w = call(
        cross_project_kernel,
        [shape((8, 896), F32), shape((8, 256, 256), BF)],
        (pos, summaries, *cross_w),
        flops=10**8,
        moved=3 * 2**20,
    )
    cross_got = lax.ppermute(cross_part, "seq", CORE)
    (rows,) = call(
        cross_scale_kernel, [shape((16, 8, 768), BF)], (cross_part, cross_got), moved=10**6
    )
    same_core = [[i * 2 + k for i in range(16)] for k in range(2)]
    gathered = lax.all_to_all(rows, "seq", 0, 0, axis_index_groups=same_core)
    cross_mixed, update = call(
        cross_attend_kernel,
        [shape((128, 256), BF), shape((8, 8, 256), F32)],
        (pos, gathered, back_w),
        scratch=[pltpu.VMEM((128, 256), F32)],
        flops=10**8,
        moved=10**6,
    )
    parts = lax.all_to_all(update, "tp", 0, 0)
    mine, theirs = call(
        update_kernel, [shape((8, 256), F32), shape((8, 256), F32)], (pos, parts), moved=10**5
    )
    got_update = lax.ppermute(theirs, "seq", CORE)
    layer_out, cross_update = call(
        final_kernel,
        [shape((per, cols), BF), shape((segs, cols), F32)],
        (pos, valid, seg_mine, seg_take, mine, got_update),
        flops=10**6,
        moved=10**6,
    )
    (grad_weight,) = call(
        grad_kernel,
        [shape((256, 128), F32)],
        (cross_mixed, summaries),
        flops=10**7,
        moved=10**5,
    )
    return (layer_out, cross_update, grad_weight)


def solution(mesh):
    return jax.shard_map(
        local,
        mesh=mesh,
        in_specs=(
            P("seq", "tp"),
            P("seq"),
            P("seq", "tp"),
            P("seq", "tp"),
            P("seq", "tp"),
            P("tp", "seq"),
            P("seq", "tp"),
            P("seq", "tp"),
            P("seq", "tp"),
            P("tp", "seq"),
            P("seq", "tp"),
        ),
        out_specs=(P("seq", "tp"), P("seq", "tp"), P("tp", "seq")),
        check_vma=False,
    )
```

```python
import jax
import jax.numpy as jnp
from jax import lax
from jax.experimental import pallas as pl
from jax.experimental.pallas import tpu as pltpu
from jax.sharding import PartitionSpec as P

HD = 128
SEG = 128
EPS = 1e-05
NZ = 8
NY = 4
BF = jnp.bfloat16
F32 = jnp.float32
VMEM = pl.BlockSpec(memory_space=pltpu.VMEM)
SMEM = pl.BlockSpec(memory_space=pltpu.SMEM)

CORE = [(i, i ^ 1) for i in range(32)]
XHI = [(i, i ^ 2) for i in range(32)]
XLO = [(i, i ^ 1) for i in range(8)]


def along_z(step):
    return [(i, (i + 4 * step) % 32) for i in range(32)]


def along_y(step):
    return [(i, (i + 2 * step) % 8) for i in range(8)]


def call(body, outs, args, scratch=(), flops=0, moved=0):
    specs = [SMEM if a.dtype == jnp.int32 else VMEM for a in args]
    return pl.pallas_call(
        body,
        out_shape=outs,
        in_specs=specs,
        out_specs=[VMEM] * len(outs),
        scratch_shapes=list(scratch),
        compiler_params=pltpu.CompilerParams(vmem_limit_bytes=16 * 2**20),
        cost_estimate=pl.CostEstimate(flops=flops, bytes_accessed=moved, transcendentals=0),
    )(*args)


def shape(dims, dtype):
    return jax.ShapeDtypeStruct(dims, dtype)


def dot(a, b):
    return jnp.dot(a, b, preferred_element_type=F32)


def tie(*arrays):
    return lax.optimization_barrier(arrays)


def in_order(flag, mine, other, axis):
    return jnp.concatenate(
        [jnp.where(flag, mine, other), jnp.where(flag, other, mine)], axis=axis
    )


def assemble_kernel(pos, p0, p1, p2a, p2b, p3, x_out, own_sq, sib_sq):
    x_hi, core = pos[1], pos[2]
    rows = p0.shape[1]
    per = rows // 2
    low = x_hi == 0
    pieces = [p0.at[0], p0.at[1], p1.at[0], p1.at[1], p2a, p2b, p3.at[0], p3.at[1]]
    for k in range(8):
        left, right = pieces[k][:, :128], pieces[k][:, 128:]
        x_out[k, :, :128] = jnp.where(low, left, right)
        x_out[k, :, 128:] = jnp.where(low, right, left)
    segs = per // SEG
    for which, ref in ((0, own_sq), (1, sib_sq)):
        base = pl.multiple_of((core if which == 0 else 1 - core) * per, per)
        for j in range(segs):
            at = pl.ds(base + j * SEG, SEG)
            total = jnp.zeros((SEG, 128), F32)
            for k in range(8):
                v = x_out[k, at, :].astype(F32)
                total += v[:, :128] * v[:, :128] + v[:, 128:] * v[:, 128:]
            ref[j * SEG : (j + 1) * SEG, :] = jnp.broadcast_to(
                jnp.sum(total, axis=1, keepdims=True), (SEG, 128)
            )


def project_kernel(pos, x, own0, far0, u1, d1, u2, d2, u3, d3, u4, d4, u5, d5, own, sib, w):
    z, core, y = pos[0], pos[2], pos[3]
    per = own.shape[0]
    w[0, 0:128, :] = own0[...]
    w[0, 128:256, :] = far0[...]
    w[7, 0:128, :] = u1[...]
    w[1, 0:128, :] = d1[...]
    w[6, 0:128, :] = u2[0:128, :]
    w[7, 128:256, :] = u2[128:256, :]
    w[2, 0:128, :] = d2[128:256, :]
    w[1, 128:256, :] = d2[0:128, :]
    w[5, 0:128, :] = u3[0:128, :]
    w[6, 128:256, :] = u3[128:256, :]
    w[3, 0:128, :] = d3[128:256, :]
    w[2, 128:256, :] = d3[0:128, :]
    w[4, 64:128, :] = u4[0:64, :]
    w[5, 128:256, :] = u4[64:192, :]
    w[4, 0:64, :] = d4[128:192, :]
    w[3, 128:256, :] = d4[0:128, :]
    w[4, 192:256, :] = u5[...]
    w[4, 128:192, :] = d5[...]
    for which, ref in ((1, sib), (0, own)):
        base = pl.multiple_of((core if which == 0 else 1 - core) * per, per)
        for j in range(per // SEG):
            at = pl.ds(base + j * SEG, SEG)
            total = None
            for k in range(8):
                term = dot(x[lax.rem(z + k - 2 * y + 16, 8), at, :], w[k])
                total = term if total is None else total + term
            ref[j * SEG : (j + 1) * SEG, :] = total.astype(ref.dtype)


def attend_kernel(valid, own, got, own_sq, got_sq, out, mixed):
    heads = mixed.shape[1] // HD
    width = heads * HD
    features = 4096.0
    for j in range(own.shape[0] // SEG):
        at = slice(j * SEG, (j + 1) * SEG)
        scale = lax.rsqrt((own_sq[at, :] + got_sq[at, :]) * (1.0 / features) + EPS)
        allowed = lax.broadcasted_iota(jnp.int32, (SEG, SEG), 1) < valid[j]
        for h in range(heads):
            parts = []
            for kind in range(3):
                cols = slice(kind * width + h * HD, kind * width + (h + 1) * HD)
                parts.append(((own[at, cols] + got[at, cols].astype(F32)) * scale).astype(BF))
            q, k, v = parts
            scores = lax.dot_general(
                q, k, (((1,), (1,)), ((), ())), preferred_element_type=F32
            ) * (HD**-0.5)
            scores = jnp.where(allowed, scores, -1e30)
            weights = jnp.exp(scores - jnp.max(scores, axis=1, keepdims=True))
            weights = (weights / jnp.sum(weights, axis=1, keepdims=True)).astype(BF)
            part = dot(weights, v).astype(BF)
            mixed[at, h * HD : (h + 1) * HD] = part
    for to in range(out.shape[0]):
        out[to] = mixed[...]


def out_kernel(pos, chip, own, sib, grads, *refs):
    w, (mine, theirs, summary, rows) = refs[:9], refs[9:]
    z, core = pos[0], pos[2]
    per = mine.shape[0]
    part = per // 2
    segs = per // SEG
    rows[...] = jnp.zeros_like(rows)
    for which, src, ref in ((0, own, mine), (1, sib, theirs)):
        chip_core = core if which == 0 else 1 - core
        for h in range(2):
            at = slice(h * part, (h + 1) * part)
            total = None
            for k in range(8):
                weights = w[k if k < 4 else k + 1]
                last = weights.shape[1]
                term = dot(src[lax.rem(z + k, 8), at, :], weights[:, last - 256 : last])
                total = term if total is None else total + term
            base = pl.multiple_of(chip_core * per + h * part, part)
            sums = (chip[pl.ds(base, part), :].astype(F32) + total).astype(BF)
            ref[at, :] = sums
            for j in range(segs):
                place = j * SEG - h * part
                if 0 <= place < part:
                    row = sums[place : place + 16, :].astype(F32)[0:1]
                    rows[pl.ds(chip_core * segs + j, 1), :] = row
    for to in range(summary.shape[0]):
        summary[to, 0:8, :] = rows[...]
        summary[to, 8:16, :] = grads[...]


def cross_project_kernel(pos, rows, *refs):
    w, out, table = refs[:9], refs[9], refs[10]
    z = pos[0]
    width = out.shape[1] - 128
    half = w[4].shape[1]
    total = jnp.zeros((8, width), F32)
    square = jnp.zeros((8, 128), F32)
    for k in range(8):
        at = lax.rem(z + k, 8)
        wide = rows[at, 0:8, :]
        ref = w[k if k < 4 else k + 1]
        table[at] = ref[:, ref.shape[1] - 512 : ref.shape[1] - 256]
        square += wide[:, :128] * wide[:, :128] + wide[:, 128:] * wide[:, 128:]
        wide = wide.astype(BF)
        if k == 4:
            total += jnp.concatenate(
                [dot(wide, w[4][...]), dot(wide, w[5][:, : width - half])], axis=1
            )
        else:
            total += dot(wide, ref[:, :width])
    out[:, :width] = total
    out[:, width:] = jnp.broadcast_to(jnp.sum(square, axis=1, keepdims=True), (8, 128))


def cross_scale_kernel(own, got, out):
    width = own.shape[1] - 128
    scale = lax.rsqrt((own[:, width:] + got[:, width:]) * (1.0 / 4096.0) + EPS)
    for k in range(width // 128):
        cols = slice(k * 128, (k + 1) * 128)
        block = ((own[:, cols] + got[:, cols]) * scale).astype(BF)
        for to in range(out.shape[0]):
            out[to, :, cols] = block


def cross_attend_kernel(pos, gathered, w, mixed, update, table):
    z, x_hi = pos[0], pos[1]
    count = gathered.shape[0] * 8
    rows = gathered[...].astype(F32).reshape(count, gathered.shape[2]).astype(BF)
    width = rows.shape[1] // 3
    key_index = lax.broadcasted_iota(jnp.int32, (count, count), 1)
    allowed = key_index % 8 < 6
    for h in range(width // HD):
        q = rows[:, h * HD : (h + 1) * HD]
        k = rows[:, width + h * HD : width + (h + 1) * HD]
        v = rows[:, 2 * width + h * HD : 2 * width + (h + 1) * HD]
        scores = lax.dot_general(
            q, k, (((1,), (1,)), ((), ())), preferred_element_type=F32
        ) * (HD**-0.5)
        scores = jnp.where(allowed, scores, -1e30)
        weights = jnp.exp(scores - jnp.max(scores, axis=1, keepdims=True))
        weights = (weights / jnp.sum(weights, axis=1, keepdims=True)).astype(BF)
        table[:, h * HD : (h + 1) * HD] = dot(weights, v)
    mixed[...] = table[...].astype(BF)
    chip = table[pl.ds(pl.multiple_of((z * 2 + x_hi) * 8, 8), 8), :].astype(BF)
    for k in range(8):
        update[k] = dot(chip, w[k])


def update_kernel(pos, parts, mine, theirs):
    core = pos[2]
    total = parts[0]
    for k in range(1, parts.shape[0]):
        total = total + parts[k]
    later = jnp.concatenate([total[3:], total[:3]], axis=0)
    mine[...] = jnp.where(core == 0, total, later)
    theirs[...] = jnp.where(core == 0, later, total)


def final_kernel(pos, valid, seg_mine, seg_theirs, mine, theirs, out, update):
    core = pos[2]
    segs = update.shape[0]
    place = lax.broadcasted_iota(jnp.int32, (SEG, 1), 0)
    for which, seg, ref in ((0, seg_mine, mine), (1, seg_theirs, theirs)):
        part = core if which == 0 else 1 - core
        for x in range(2):
            cols = pl.ds(pl.multiple_of(x * 256 + part * 128, 128), 128)
            from_cols = slice(x * 128, (x + 1) * 128)
            update[:, cols] = ref[:segs, from_cols]
            for j in range(segs):
                at = slice(j * SEG, (j + 1) * SEG)
                live = (place < valid[j]).astype(F32)
                sums = seg[at, from_cols].astype(F32) + ref[j : j + 1, from_cols]
                out[at, cols] = (sums * live).astype(BF)


def grad_kernel(mixed, grads, out):
    total = jnp.zeros(out.shape, F32)
    for k in range(8):
        block = grads[k, 8:16, :]
        right = jnp.concatenate([block[:, :128], block[:, 128:]], axis=0).astype(BF)
        total += lax.dot_general(
            mixed[k * 16 : (k + 1) * 16, :], right, (((0,), (0,)), ((), ())),
            preferred_element_type=F32,
        )
    out[...] = total


def local(
    tokens, valid, seg_query, seg_key, seg_value, seg_output,
    cross_query, cross_key, cross_value, cross_output, cotangent,
):
    per, cols = tokens.shape
    segs = per // SEG
    s = lax.axis_index("seq")
    t = lax.axis_index("tp")
    z, x_hi, core = s // 4, (s // 2) % 2, s % 2
    y, x_lo = t // 2, t % 2
    pos = jnp.stack([z, x_hi, core, y, x_lo]).astype(jnp.int32)
    is0 = core == 0

    at0 = x_hi == 0
    low = x_lo == 0
    swap = [
        (i * 8 + j, (j * 4 + i % 4) * 8 + i // 4) for i in range(32) for j in range(8)
    ]


    def z_step(block, step):
        return lax.ppermute(block, "seq", along_z(step))

    def y_step(block, step):
        return lax.ppermute(block, "tp", along_y(step))

    four = tokens.reshape(per, 2, 2, 128)
    keep = jnp.where(is0, four[:, :, 0], four[:, :, 1]).reshape(per, 256)
    give = jnp.where(is0, four[:, :, 1], four[:, :, 0]).reshape(per, 256)
    block = jnp.concatenate([seg_query, seg_key, seg_value], axis=1)
    cross_block = jnp.concatenate([cross_query, cross_key, cross_value], axis=1)
    far = lax.ppermute(block, "seq", XHI)
    take = lax.ppermute(give, "seq", CORE)
    live = jnp.arange(SEG, dtype=jnp.int32)[None, :] < valid[:, None]
    keep_rows = live.astype(F32)[:, :, None]
    grad = jnp.sum(cotangent.astype(F32).reshape(segs, SEG, cols) * keep_rows, axis=1)
    grad = jnp.pad(grad.astype(BF), ((0, 1), (0, 0))).reshape(16, 128)
    turned = lax.ppermute(jnp.concatenate([seg_output, grad], axis=0), ("seq", "tp"), swap)
    u1, d1 = z_step(block, 1), z_step(block, -1)
    far, take, u1, d1 = tie(far, take, u1, d1)

    chip = in_order(is0, keep, take, 0)
    chip_x = lax.ppermute(chip, "tp", XLO)
    up1 = z_step(jnp.concatenate([u1, far], axis=0), 1)
    down1 = z_step(jnp.concatenate([far, d1], axis=0), -1)
    up1, down1, chip_x = tie(up1, down1, chip_x)

    up2, down2 = z_step(up1, 1), z_step(down1, -1)
    p0 = in_order(low, chip[None], chip_x[None], 0)
    p3, p1 = y_step(p0, 1), y_step(p0, -1)
    grad = turned[256:].reshape(segs + 1, 2, 2, 128)[:segs]
    g_keep = jnp.where(is0, grad[:, :, 0], grad[:, :, 1])
    g_take = lax.ppermute(jnp.where(is0, grad[:, :, 1], grad[:, :, 0]), "seq", CORE)
    up2, down2, g_take, turned, cross_block, cross_output = tie(
        up2, down2, g_take, turned, cross_block, cross_output
    )

    up3, down3 = z_step(up2[64:], 1), z_step(down2[:192], -1)
    g_chip = jnp.concatenate(
        [in_order(is0, g_keep, g_take, 0), jnp.zeros((8 - 2 * segs, 2, 128), BF)]
    )
    g_own = jnp.where(at0, g_chip[:, 0], g_chip[:, 1])
    g_give = jnp.where(at0, g_chip[:, 1], g_chip[:, 0])
    cross_pack = jnp.concatenate(
        [cross_block, cross_output[:128], cross_output[128:], turned[:128], turned[128:256]],
        axis=1,
    )
    cross_far = lax.ppermute(
        jnp.concatenate([cross_pack, jnp.pad(g_give, ((0, 8), (0, 1152)))], axis=0), "seq", XHI
    )
    up3, down3, cross_far, p3, p1 = tie(up3, down3, cross_far, p3, p1)
    g_rows = in_order(at0, g_own, cross_far[128:136, :128], 1).astype(F32)
    cross_far = cross_far[:128]

    def tall(wide):
        return jnp.concatenate([wide[:, :128], wide[:, 128:]], axis=0)

    cross_plane = jnp.concatenate(
        [
            in_order(at0, cross_block, cross_far[:, :768], 0),
            in_order(at0, cross_output, tall(cross_far[:, 768:1024]), 1),
            in_order(at0, turned[:256], tall(cross_far[:, 1024:]), 1),
        ],
        axis=1,
    )

    up4, down4 = z_step(up3[128:], 1), z_step(down3[:64], -1)
    p2a, p2b = y_step(p3[0], 1), y_step(p1[1], -1)
    p2a, cross_plane = tie(p2a, cross_plane)
    c_up1, c_down1 = z_step(cross_plane, 1), z_step(cross_plane, -1)
    up4, down4, p2a, p2b = tie(up4, down4, p2a, p2b)

    x, own_sq, sib_sq = call(
        assemble_kernel,
        [shape((8, 2 * per, 256), BF), shape((per, 128), F32), shape((per, 128), F32)],
        (pos, p0, p1, p2a, p2b, p3),
        moved=8 * 2**20,
    )
    got_sq = lax.ppermute(sib_sq, "seq", CORE)
    own_p, sib_p = call(
        project_kernel,
        [shape((per, 768), F32), shape((per, 768), BF)],
        (pos, x, block, far, u1, d1, up1, down1, up2, down2, up3, down3, up4, down4),
        scratch=[pltpu.VMEM((8, 256, 768), BF)],
        flops=2 * 768 * 768 * 2048,
        moved=8 * 2**20,
    )
    got_p = lax.ppermute(sib_p, "seq", CORE)
    got_p, got_sq, c_up1, c_down1 = tie(got_p, got_sq, c_up1, c_down1)
    c_up2, c_down2 = z_step(c_up1, 1), z_step(c_down1, -1)
    (mixed,) = call(
        attend_kernel,
        [shape((8, per, 256), BF)],
        (valid, own_p, got_p, own_sq, got_sq),
        scratch=[pltpu.VMEM((per, 256), BF)],
        flops=10**8,
        moved=3 * 2**20,
    )

    mixed, c_up2, c_down2 = tie(mixed, c_up2, c_down2)
    c_up3, c_down3 = z_step(c_up2, 1), z_step(c_down2, -1)
    mixed = lax.all_to_all(mixed, "tp", 0, 0)
    mixed, c_up3, c_down3 = tie(mixed, c_up3, c_down3)
    half = cross_plane.shape[1] // 2
    c_up4, c_down4 = z_step(c_up3[:, :half], 1), z_step(c_down3[:, half:], -1)
    cross_w = (
        cross_plane, c_down1, c_down2, c_down3, c_up4, c_down4, c_up3, c_up2, c_up1
    )
    mixed_sib = lax.ppermute(mixed, "seq", CORE)
    seg_mine, seg_give, summary = call(
        out_kernel,
        [shape((per, 256), BF), shape((per, 256), BF), shape((8, 16, 256), F32)],
        (pos, chip, mixed, mixed_sib, g_rows, *cross_w),
        scratch=[pltpu.VMEM((8, 256), F32)],
        flops=2 * per * 512 * 2048,
        moved=6 * 2**20,
    )
    summaries = lax.all_to_all(summary, "tp", 0, 0)
    seg_take = lax.ppermute(seg_give, "seq", CORE)

    cross_part, back_w = call(
        cross_project_kernel,
        [shape((8, 896), F32), shape((8, 256, 256), BF)],
        (pos, summaries, *cross_w),
        flops=10**8,
        moved=3 * 2**20,
    )
    cross_got = lax.ppermute(cross_part, "seq", CORE)
    (rows,) = call(
        cross_scale_kernel, [shape((16, 8, 768), BF)], (cross_part, cross_got), moved=10**6
    )
    same_core = [[i * 2 + k for i in range(16)] for k in range(2)]
    gathered = lax.all_to_all(rows, "seq", 0, 0, axis_index_groups=same_core)
    cross_mixed, update = call(
        cross_attend_kernel,
        [shape((128, 256), BF), shape((8, 8, 256), F32)],
        (pos, gathered, back_w),
        scratch=[pltpu.VMEM((128, 256), F32)],
        flops=10**8,
        moved=10**6,
    )
    parts = lax.all_to_all(update, "tp", 0, 0)
    mine, theirs = call(
        update_kernel, [shape((8, 256), F32), shape((8, 256), F32)], (pos, parts), moved=10**5
    )
    got_update = lax.ppermute(theirs, "seq", CORE)
    layer_out, cross_update = call(
        final_kernel,
        [shape((per, cols), BF), shape((segs, cols), F32)],
        (pos, valid, seg_mine, seg_take, mine, got_update),
        flops=10**6,
        moved=10**6,
    )
    (grad_weight,) = call(
        grad_kernel,
        [shape((256, 128), F32)],
        (cross_mixed, summaries),
        flops=10**7,
        moved=10**5,
    )
    return (layer_out, cross_update, grad_weight)


def solution(mesh):
    return jax.shard_map(
        local,
        mesh=mesh,
        in_specs=(
            P("seq", "tp"),
            P("seq"),
            P("seq", "tp"),
            P("seq", "tp"),
            P("seq", "tp"),
            P("tp", "seq"),
            P("seq", "tp"),
            P("seq", "tp"),
            P("seq", "tp"),
            P("tp", "seq"),
            P("seq", "tp"),
        ),
        out_specs=(P("seq", "tp"), P("seq", "tp"), P("tp", "seq")),
        check_vma=False,
    )
```
